32 devices in a mesh: dp: 8 (over z, x), tp: 4 (over y, core).
Axes of the slice: x: 2, y: 2, z: 4, core: 2. Of those that a mesh axis runs over, the one named last changes fastest.
Arguments:
- queries: bfloat16 [64, 128, 576], P(('dp', 'tp')), may hold values from -40 to 40
- latent_cache: bfloat16 [64, 256, 576], P(('dp', 'tp')), may hold values from -5 to 5
- lengths: int32 [64], P(('dp', 'tp')), may hold values from 1 to 256, 4096 in all
- value_weight: bfloat16 [128, 512, 128], P('tp'), may hold values from -0.25 to 0.25
- output_weight: bfloat16 [16384, 7168], P('tp', 'dp'), may hold values from -0.046875 to 0.046875
Outputs:
- attended: bfloat16 [64, 7168], P(('dp', 'tp'))
The draws below stay inside these ranges and needn't reach their ends.
All inputs are finite; a program needn't handle non-finite values. No bound on the sum of `lengths` on one device may be relied on, other than what follows from the above.
Results may differ from the reference program's by a relative error of at most 0.0065.
Values may be sent and summed in bfloat16 or wider, within the bound.
A program may use at most 64 MiB of HBM per device.

```python
import math
import jax
import jax.numpy as jnp
import numpy as np
from jax import lax

H = 128
DL = 512
DR = 64
DV = 128
D = 7168
REQ_DEV = 2
LMAX = 256
REQS = 64


def clipped_normal(key, shape):
    return jnp.clip(jax.random.normal(key, shape, jnp.float32), -4.0, 4.0)


def first_slots(key):
    return clipped_normal(jax.random.fold_in(key, 105), (REQS, DL + DR))


def draw_latent_cache(key, part):
    base = clipped_normal(jax.random.fold_in(key, 101), (REQS, LMAX, DL + DR))
    base = base.at[:, 0, :].set(first_slots(key))
    return base.astype(jnp.bfloat16)


def draw_queries(key, part):
    base = clipped_normal(jax.random.fold_in(key, 104), (REQS, H, DL + DR))
    return base.astype(jnp.bfloat16)


def levels(key, extent, split, low, top_value):
    def one(position, shards_of):
        draws = jax.random.uniform(jax.random.fold_in(jax.random.fold_in(key, 6), position), (shards_of,), jnp.float32, low / len(split), top_value / len(split))
        return jnp.repeat(jnp.exp(draws), extent[position] // shards_of).reshape((-1,) + (1,) * (len(extent) - position - 1))

    level = one(*split[0])
    for cut in split[1:]:
        level = level * one(*cut)
    return level


def split_up(amount, total, limit, lean):
    portions = [(1 << 20) // math.isqrt(grade ** lean) + 1 for grade in range(2, amount + 1)]
    surplus, counts = total - limit - (amount - 1), [1] * (amount - 1)
    while surplus > 0:
        free = [i for i in range(amount - 1) if counts[i] < limit]
        pool, remaining = sum([portions[i] for i in free]), surplus
        for i in free:
            more = min(limit - counts[i], max(1, remaining * portions[i] // pool), surplus)
            counts[i] = counts[i] + more
            surplus = surplus - more
    return np.array([limit] + counts)


def uneven_parts(rng, amount, total, reach, skew):
    if amount == 2:
        one = jax.random.randint(rng, (), max(1, total - reach), min(reach, total - 1) + 1)
        return jnp.stack([one, total - one])
    tallies = jnp.asarray(split_up(amount, total, reach, skew), jnp.int32)
    couples = (amount - 1) // 2
    giver, taker = tallies[1:1 + 2 * couples:2], tallies[2:2 + 2 * couples:2]
    slack = jnp.minimum(giver - 1, reach - taker)
    moved = jax.random.randint(jax.random.fold_in(rng, 1), (couples,), 0, 1 << 20) % (slack + 1)
    tallies = tallies.at[1:1 + 2 * couples:2].set(giver - moved).at[2:2 + 2 * couples:2].set(taker + moved)
    return tallies[jax.random.permutation(jax.random.fold_in(rng, 2), amount)]


def normal_values(rng, dims, spread, limit, pieces=(), kind=jnp.bfloat16):
    entries = jax.random.normal(rng, dims, jnp.float32) * spread
    if len(pieces) > 0:
        entries = levels(rng, dims, pieces, -0.22, 0.18) * entries
    return jnp.clip(entries, min=-limit, max=limit).astype(kind)


def setup_inputs(seed: int = 0) -> dict:
    streams_of = jax.random.split(jax.random.key(seed), 6)
    queries = draw_queries(jax.random.fold_in(streams_of[5], 71), 0)
    latent_cache = draw_latent_cache(jax.random.fold_in(streams_of[5], 71), 0)
    lengths = uneven_parts(streams_of[2], REQS, REQS * LMAX // 4, LMAX, 2).astype(jnp.int32)
    value_weight = normal_values(streams_of[3], (H, DL, DV), DL ** -0.5, 0.25, ((0, 4),))
    output_weight = normal_values(streams_of[4], (H * DV, D), (H * DV) ** -0.5, 0.046875, ((0, 4), (1, 8)))
    return dict(queries=queries, latent_cache=latent_cache, lengths=lengths, value_weight=value_weight, output_weight=output_weight)


score_scale = 192.0 ** -0.5


def attend_block(queries, latent_cache, lengths, value_weight):
    scores = jnp.einsum("rhe,rje->rhj", queries.astype(jnp.float32), latent_cache.astype(jnp.float32)) * score_scale
    alive = jnp.arange(latent_cache.shape[1], dtype=jnp.int32)[None, None, :] < lengths[:, None, None]
    scores = jnp.where(alive, scores, -1e30)
    row_max = jnp.max(scores, axis=2, keepdims=True)
    powers = jnp.exp(scores - row_max)
    weights = (powers / jnp.sum(powers, axis=2, keepdims=True)).astype(jnp.bfloat16)
    mixture = jnp.einsum("rhj,rje->rhe", weights.astype(jnp.float32), latent_cache.astype(jnp.float32))
    latent = mixture[:, :, :DL].astype(jnp.bfloat16)
    values = jnp.einsum("rhd,hde->rhe", latent.astype(jnp.float32), value_weight.astype(jnp.float32))
    return values.astype(jnp.bfloat16)


def reference(queries, latent_cache, lengths, value_weight, output_weight):
    block_count = REQS // REQ_DEV
    stacked_queries = queries.reshape(block_count, REQ_DEV, H, DL + DR)
    stacked_cache = latent_cache.reshape(block_count, REQ_DEV, LMAX, DL + DR)
    stacked_lengths = lengths.reshape(block_count, REQ_DEV)

    def one_block(item):
        return attend_block(item[0], item[1], item[2], value_weight)

    values = lax.map(one_block, (stacked_queries, stacked_cache, stacked_lengths))
    values = values.reshape(REQS, H * DV)
    return jnp.dot(values, output_weight, preferred_element_type=jnp.float32).astype(jnp.bfloat16)
```

```python
import functools

import jax
import jax.numpy as jnp
from jax import lax
from jax.experimental import pallas as pl
from jax.experimental.pallas import tpu as pltpu
from jax.sharding import PartitionSpec as P

score_scale = 192.0 ** (-0.5)
MESH = pl.DeviceIdType.MESH
chunk_count = 2


def attend(query_t, cache_t, length, latent_width):
    scores = (
        lax.dot_general(
            query_t, cache_t, (((0,), (0,)), ((), ())), preferred_element_type=jnp.float32
        )
        * score_scale
    )
    alive = lax.broadcasted_iota(jnp.int32, scores.shape, 1) < length
    scores = jnp.where(alive, scores, -1e30)
    powers = jnp.exp(scores - jnp.max(scores, axis=1, keepdims=True))
    weights = (powers / jnp.sum(powers, axis=1, keepdims=True)).astype(jnp.bfloat16)
    latent = lax.dot_general(
        weights,
        cache_t[:latent_width],
        (((1,), (1,)), ((), ())),
        preferred_element_type=jnp.float32,
    )
    return latent.astype(jnp.bfloat16)


def kernel(
    lengths_ref,
    query_hbm,
    cache_hbm,
    value_hbm,
    output_hbm,
    out_ref,
    query,
    cache,
    value_weight,
    output_weight,
    latent_out,
    latent_in,
    latent_wide,
    gathered,
    total,
    partial,
    partial_in,
    piece,
    piece_in,
    load_sem,
    b_send,
    b_recv,
    d_send,
    d_recv,
    f_send,
    f_recv,
    g_send,
    g_recv,
):
    dp = lax.axis_index("dp")
    tp = lax.axis_index("tp")
    requests, groups, heads, latent_width = latent_out.shape
    chunks, columns, rows2, lanes = gathered.shape
    value_width = value_weight.shape[2]
    half = heads // 2
    per_chunk = half // chunks
    width = output_weight.shape[1]
    rows = groups * requests

    tp_peers = [None, tp + 1 - 2 * lax.rem(tp, 2), lax.rem(tp + 2, 4), 3 - tp]
    across = dp + 1 - 2 * lax.rem(dp, 2)

    loads = []
    for q in range(requests):
        loads.append(pltpu.make_async_copy(cache_hbm.at[q], cache.at[q], load_sem.at[2 * q]))
        loads.append(pltpu.make_async_copy(query_hbm.at[q], query.at[q], load_sem.at[2 * q + 1]))
    load_value = pltpu.make_async_copy(value_hbm, value_weight, load_sem.at[2 * requests])
    load_output = pltpu.make_async_copy(output_hbm, output_weight, load_sem.at[2 * requests + 1])
    for copy in loads:
        copy.start()
    load_value.start()
    load_output.start()

    barrier = pltpu.get_barrier_semaphore()
    for d in (1, 2, 3):
        pl.semaphore_signal(barrier, inc=1, device_id=(dp, tp_peers[d]), device_id_type=MESH)
    for d in range(1, columns):
        pl.semaphore_signal(
            barrier, inc=1, device_id=(lax.rem(dp + d, columns), tp), device_id_type=MESH
        )

    b_copies = []
    for q in range(requests):
        loads[2 * q].wait()
        loads[2 * q + 1].wait()
        latent = attend(query[q], cache[q], lengths_ref[q], latent_width)
        latent_out[q] = latent.reshape(groups, heads, latent_width)
        if q == 0:
            pl.semaphore_wait(barrier, groups - 1 + columns - 1)
        for d in (2, 3, 1):
            copy = pltpu.make_async_remote_copy(
                src_ref=latent_out.at[q, tp_peers[d]],
                dst_ref=latent_in.at[d, q],
                send_sem=b_send.at[q, d],
                recv_sem=b_recv.at[q, d],
                device_id=(dp, tp_peers[d]),
                device_id_type=MESH,
            )
            copy.start()
            b_copies.append((d, q, copy))

    def widen(block, k, q):
        first = pl.multiple_of((k * requests + q) * heads, heads)
        for b in range(latent_width // 128):
            latent_wide[b, pl.ds(first, heads), :] = block[:, b * 128 : (b + 1) * 128].astype(
                jnp.float32
            )

    for q in range(requests):
        widen(latent_out.at[q, tp], tp, q)
    for d, q, copy in sorted(b_copies, key=lambda item: (item[0] != 1, item[1], item[0])):
        copy.wait_recv()
        widen(latent_in.at[d, q], tp_peers[d], q)

    load_value.wait()

    def project(head):
        rows_of = jnp.concatenate(
            [
                latent_wide[b, pl.ds(head, rows, stride=heads), :]
                for b in range(latent_width // 128)
            ],
            axis=1,
        )
        return jnp.dot(
            rows_of.astype(jnp.bfloat16), value_weight[head], preferred_element_type=jnp.float32
        )

    def value_copy(c, s, slot, device):
        return pltpu.make_async_remote_copy(
            src_ref=gathered.at[c, s],
            dst_ref=gathered.at[c, s],
            send_sem=d_send.at[c, slot],
            recv_sem=d_recv.at[c, slot],
            device_id=(device, tp),
            device_id_type=MESH,
        )

    d_copies = []
    for c in range(chunks):
        for i in range(per_chunk):
            head = c * per_chunk + i
            pair = jnp.concatenate([project(head), project(half + head)], axis=0)
            gathered[c, dp, :, i * value_width : (i + 1) * value_width] = pair.astype(jnp.bfloat16)
        for dz in (2, 1, 3):
            copy = value_copy(c, dp, dz, lax.rem(dp + 2 * dz, columns))
            copy.start()
            d_copies.append(copy)
        copy = value_copy(c, dp, 0, across)
        copy.start()
        d_copies.append(copy)

    load_output.wait()
    depth = half * value_width
    for c in range(chunks):
        for dz in (1, 3, 2):
            source = lax.rem(dp + columns - 2 * dz, columns)
            value_copy(c, source, dz, across).wait_recv()
            copy = value_copy(c, source, 3 + dz, across)
            copy.start()
            d_copies.append(copy)
        for slot in (0, 4, 6, 5):
            value_copy(c, across, slot, across).wait_recv()
        block = gathered[c].reshape(columns * rows2, lanes)
        low = jnp.dot(
            block,
            output_weight[c * lanes : (c + 1) * lanes],
            preferred_element_type=jnp.float32,
        )
        high = jnp.dot(
            block,
            output_weight[depth + c * lanes : depth + (c + 1) * lanes],
            preferred_element_type=jnp.float32,
        )
        low = low.reshape(columns, rows2, width)[:, :rows]
        high = high.reshape(columns, rows2, width)[:, rows:]
        term = (low + high).reshape(columns * rows, width)
        for b in range(width // 128):
            if c == 0:
                total[b] = term[:, b * 128 : (b + 1) * 128]
            else:
                total[b] += term[:, b * 128 : (b + 1) * 128]

    def rows_for(k):
        return jnp.concatenate(
            [
                jnp.concatenate(
                    [
                        total[b, pl.ds(k * requests + q, columns, stride=rows), :]
                        for b in range(width // 128)
                    ],
                    axis=1,
                )
                for q in range(requests)
            ],
            axis=0,
        )

    f_copies = []
    for d in (2, 3, 1):
        partial[d] = rows_for(tp_peers[d]).astype(partial.dtype)
        copy = pltpu.make_async_remote_copy(
            src_ref=partial.at[d],
            dst_ref=partial_in.at[d],
            send_sem=f_send.at[d],
            recv_sem=f_recv.at[d],
            device_id=(dp, tp_peers[d]),
            device_id_type=MESH,
        )
        copy.start()
        f_copies.append((d, copy))
    summed = rows_for(tp)
    for d, copy in reversed(f_copies):
        copy.wait_recv()
        summed = summed + partial_in[d].astype(jnp.float32)

    for q in range(requests):
        piece[:, q, :] = summed[q * columns : (q + 1) * columns]
    g_copies = []
    for d in (4, 3, 5, 2, 6, 1, 7):
        to = lax.rem(dp + d, columns)
        copy = pltpu.make_async_remote_copy(
            src_ref=piece.at[to],
            dst_ref=piece_in.at[dp],
            send_sem=g_send.at[d],
            recv_sem=g_recv.at[d],
            device_id=(to, tp),
            device_id_type=MESH,
        )
        copy.start()
        g_copies.append(copy)
    piece_in[dp] = piece[dp]
    for copy in g_copies:
        copy.wait_recv()
    for i in range(columns):
        out_ref[:, i * width : (i + 1) * width] = piece_in[i].astype(out_ref.dtype)

    for _, _, copy in b_copies:
        copy.wait_send()
    for copy in d_copies:
        copy.wait_send()
    for _, copy in f_copies:
        copy.wait_send()
    for copy in g_copies:
        copy.wait_send()


def fused(queries, latent_cache, lengths, value_weight, output_weight):
    requests, all_heads, full_width = queries.shape
    slots = latent_cache.shape[1]
    groups = lax.axis_size("tp")
    columns = lax.axis_size("dp")
    heads, latent_width, value_width = value_weight.shape
    width = output_weight.shape[1]
    rows = groups * requests
    lanes = heads * value_width // 2 // chunk_count
    bf16, f32 = jnp.bfloat16, jnp.float32
    dma = pltpu.SemaphoreType.DMA
    anywhere = pl.BlockSpec(memory_space=pl.ANY)
    return pl.pallas_call(
        kernel,
        out_shape=jax.ShapeDtypeStruct((requests, columns * width), bf16),
        in_specs=[pl.BlockSpec(memory_space=pltpu.SMEM)] + [anywhere] * 4,
        out_specs=pl.BlockSpec(memory_space=pltpu.VMEM),
        scratch_shapes=[
            pltpu.VMEM((requests, full_width, all_heads), bf16),
            pltpu.VMEM((requests, full_width, slots), bf16),
            pltpu.VMEM(value_weight.shape, bf16),
            pltpu.VMEM(output_weight.shape, bf16),
            pltpu.VMEM((requests, groups, heads, latent_width), bf16),
            pltpu.VMEM((groups, requests, heads, latent_width), bf16),
            pltpu.VMEM((latent_width // 128, rows * heads, 128), f32),
            pltpu.VMEM((chunk_count, columns, 2 * rows, lanes), bf16),
            pltpu.VMEM((width // 128, columns * rows, 128), f32),
            pltpu.VMEM((groups, requests * columns, width), f32),
            pltpu.VMEM((groups, requests * columns, width), f32),
            pltpu.VMEM((columns, requests, width), f32),
            pltpu.VMEM((columns, requests, width), f32),
            dma((2 * requests + 2,)),
            dma((requests, groups)),
            dma((requests, groups)),
            dma((chunk_count, 7)),
            dma((chunk_count, 7)),
            dma((groups,)),
            dma((groups,)),
            dma((columns,)),
            dma((columns,)),
        ],
        compiler_params=pltpu.CompilerParams(
            collective_id=0, has_side_effects=True, vmem_limit_bytes=63 * 1024 * 1024
        ),
        cost_estimate=pl.CostEstimate(
            flops=2 * rows * heads * latent_width * value_width
            + 2 * rows * columns * heads * value_width * width
            + 4 * requests * all_heads * slots * full_width,
            bytes_accessed=2 * (value_weight.size + output_weight.size),
            transcendentals=requests * all_heads * slots,
        ),
    )(
        lengths,
        jnp.swapaxes(queries, 1, 2),
        jnp.swapaxes(latent_cache, 1, 2),
        value_weight,
        output_weight,
    )


def general(queries, latent_cache, lengths, value_weight, output_weight):
    latent_width = value_weight.shape[1]
    scores = (
        jnp.einsum("rhe,rje->rhj", queries, latent_cache, preferred_element_type=jnp.float32)
        * score_scale
    )
    alive_mask = lax.broadcasted_iota(jnp.int32, scores.shape, 2) < lengths[:, None, None]
    scores = jnp.where(alive_mask, scores, -1e30)
    row_max = jnp.max(scores, axis=2, keepdims=True)
    powers = jnp.exp(scores - row_max)
    weights = (powers / jnp.sum(powers, axis=2, keepdims=True)).astype(jnp.bfloat16)
    mixture = jnp.einsum("rhj,rje->rhe", weights, latent_cache, preferred_element_type=jnp.float32)
    latent = mixture[:, :, :latent_width].astype(jnp.bfloat16)
    requests = queries.shape[0]
    groups = lax.axis_size("tp")
    columns = lax.axis_size("dp")
    swapped = lax.all_to_all(latent, "tp", split_axis=1, concat_axis=0, tiled=True)
    values = jnp.einsum("nhd,hde->nhe", swapped, value_weight, preferred_element_type=jnp.float32)
    values = values.astype(jnp.bfloat16).reshape(groups, requests, -1)
    everyone = lax.all_gather(values, "dp", axis=1, tiled=True)
    all_values = everyone.reshape(groups * columns * requests, -1)
    summed = lax.psum_scatter(
        jnp.dot(all_values, output_weight, preferred_element_type=jnp.float32),
        "tp",
        scatter_dimension=0,
        tiled=True,
    )
    rounded = summed.astype(jnp.bfloat16)
    return lax.all_to_all(rounded, "dp", split_axis=0, concat_axis=1, tiled=True)


def solution(mesh):
    fits = mesh.shape["dp"] == 8 and mesh.shape["tp"] == 4
    return jax.shard_map(
        fused if fits else general,
        mesh=mesh,
        in_specs=(
            P(("dp", "tp"), None, None),
            P(("dp", "tp"), None, None),
            P(("dp", "tp")),
            P("tp", None, None),
            P("tp", "dp"),
        ),
        out_specs=P(("dp", "tp"), None),
        check_vma=False,
    )
```

```python
import functools

import jax
import jax.numpy as jnp
from jax import lax
from jax.experimental import pallas as pl
from jax.experimental.pallas import tpu as pltpu
from jax.sharding import PartitionSpec as P

score_scale = 192.0 ** (-0.5)
MESH = pl.DeviceIdType.MESH
chunk_count = 4


def attend(query, cache_t, length, latent_width):
    scores = (
        jnp.dot(query, cache_t, preferred_element_type=jnp.float32)
        * score_scale
    )
    alive = lax.broadcasted_iota(jnp.int32, scores.shape, 1) < length
    scores = jnp.where(alive, scores, -1e30)
    powers = jnp.exp(scores - jnp.max(scores, axis=1, keepdims=True))
    weights = (powers / jnp.sum(powers, axis=1, keepdims=True)).astype(jnp.bfloat16)
    latent = lax.dot_general(
        weights,
        cache_t[:latent_width],
        (((1,), (1,)), ((), ())),
        preferred_element_type=jnp.float32,
    )
    return latent.astype(jnp.bfloat16)


def kernel(
    lengths_ref,
    query_hbm,
    cache_hbm,
    value_hbm,
    output_hbm,
    out_ref,
    query,
    query_rows,
    cache,
    value_weight,
    output_weight,
    latent_out,
    latent_in,
    latent_wide,
    gathered,
    total,
    partial,
    partial_in,
    piece,
    piece_in,
    load_sem,
    b_send,
    b_recv,
    d_send,
    d_recv,
    f_send,
    f_recv,
    g_send,
    g_recv,
):
    dp = lax.axis_index("dp")
    tp = lax.axis_index("tp")
    requests, groups, heads, latent_width = latent_out.shape
    chunks, columns, rows2, lanes = gathered.shape
    value_width = value_weight.shape[2]
    half = heads // 2
    per_chunk = half // chunks
    width = output_weight.shape[1]
    rows = groups * requests

    tp_peers = [None, tp + 1 - 2 * lax.rem(tp, 2), lax.rem(tp + 2, 4), 3 - tp]
    across = dp + 1 - 2 * lax.rem(dp, 2)

    loads = []
    for q in range(requests):
        loads.append(pltpu.make_async_copy(cache_hbm.at[q], cache.at[q], load_sem.at[2 * q]))
        loads.append(pltpu.make_async_copy(query_hbm.at[q], query.at[q], load_sem.at[2 * q + 1]))
    load_value = pltpu.make_async_copy(value_hbm, value_weight, load_sem.at[2 * requests])
    load_output = pltpu.make_async_copy(output_hbm, output_weight, load_sem.at[2 * requests + 1])
    for copy in loads:
        copy.start()
    load_value.start()
    load_output.start()

    barrier = pltpu.get_barrier_semaphore()
    for d in (1, 2, 3):
        pl.semaphore_signal(barrier, inc=1, device_id=(dp, tp_peers[d]), device_id_type=MESH)
    for d in range(1, columns):
        pl.semaphore_signal(
            barrier, inc=1, device_id=(lax.rem(dp + d, columns), tp), device_id_type=MESH
        )

    b_copies = []
    for near in (False, True):
        side = tp // 2 if near else 1 - tp // 2
        first_group = side * (groups // 2)
        first_head = pl.multiple_of(first_group * heads, groups // 2 * heads)
        for q in range(requests):
            if not near:
                loads[2 * q + 1].wait()
                query_rows[q] = query[q].T
                loads[2 * q].wait()
            latent = attend(
                query_rows[q, pl.ds(first_head, groups // 2 * heads), :],
                cache[q],
                lengths_ref[q],
                latent_width,
            )
            latent_out[q, pl.ds(first_group, groups // 2)] = latent.reshape(
                groups // 2, heads, latent_width
            )
            if q == 0 and not near:
                pl.semaphore_wait(barrier, groups - 1 + columns - 1)
            for d in (1,) if near else (2, 3):
                copy = pltpu.make_async_remote_copy(
                    src_ref=latent_out.at[q, tp_peers[d]],
                    dst_ref=latent_in.at[d, q],
                    send_sem=b_send.at[q, d],
                    recv_sem=b_recv.at[q, d],
                    device_id=(dp, tp_peers[d]),
                    device_id_type=MESH,
                )
                copy.start()
                b_copies.append((d, q, copy))

    def widen(block, k, q):
        first = pl.multiple_of((k * requests + q) * heads, heads)
        for b in range(latent_width // 128):
            latent_wide[b, pl.ds(first, heads), :] = block[:, b * 128 : (b + 1) * 128].astype(
                jnp.float32
            )

    for q in range(requests):
        widen(latent_out.at[q, tp], tp, q)
    for d, q, copy in sorted(b_copies, key=lambda item: (item[0] != 1, item[1], item[0])):
        copy.wait_recv()
        widen(latent_in.at[d, q], tp_peers[d], q)

    load_value.wait()

    def project(head):
        rows_of = jnp.concatenate(
            [
                latent_wide[b, pl.ds(head, rows, stride=heads), :]
                for b in range(latent_width // 128)
            ],
            axis=1,
        )
        return jnp.dot(
            rows_of.astype(jnp.bfloat16), value_weight[head], preferred_element_type=jnp.float32
        )

    def value_copy(c, s, slot, device):
        return pltpu.make_async_remote_copy(
            src_ref=gathered.at[c, s],
            dst_ref=gathered.at[c, s],
            send_sem=d_send.at[c, slot],
            recv_sem=d_recv.at[c, slot],
            device_id=(device, tp),
            device_id_type=MESH,
        )

    d_copies = []
    for c in range(chunks):
        for i in range(per_chunk):
            head = c * per_chunk + i
            pair = jnp.concatenate([project(head), project(half + head)], axis=0)
            gathered[c, dp, :, i * value_width : (i + 1) * value_width] = pair.astype(jnp.bfloat16)
        for dz in (2, 1, 3):
            copy = value_copy(c, dp, dz, lax.rem(dp + 2 * dz, columns))
            copy.start()
            d_copies.append(copy)
        copy = value_copy(c, dp, 0, across)
        copy.start()
        d_copies.append(copy)

    load_output.wait()
    depth = half * value_width

    def hand_on(c):
        for dz in (1, 3, 2):
            source = lax.rem(dp + columns - 2 * dz, columns)
            value_copy(c, source, dz, across).wait_recv()
            copy = value_copy(c, source, 3 + dz, across)
            copy.start()
            d_copies.append(copy)

    hand_on(0)
    for c in range(chunks):
        if c + 1 < chunks:
            hand_on(c + 1)
        for slot in (0, 4, 6, 5):
            value_copy(c, across, slot, across).wait_recv()
        block = gathered[c].reshape(columns * rows2, lanes)
        low = jnp.dot(
            block,
            output_weight[c * lanes : (c + 1) * lanes],
            preferred_element_type=jnp.float32,
        )
        high = jnp.dot(
            block,
            output_weight[depth + c * lanes : depth + (c + 1) * lanes],
            preferred_element_type=jnp.float32,
        )
        low = low.reshape(columns, rows2, width)[:, :rows]
        high = high.reshape(columns, rows2, width)[:, rows:]
        term = (low + high).reshape(columns * rows, width)
        for b in range(width // 128):
            if c == 0:
                total[b] = term[:, b * 128 : (b + 1) * 128]
            else:
                total[b] += term[:, b * 128 : (b + 1) * 128]

    def rows_for(k):
        return jnp.concatenate(
            [
                jnp.concatenate(
                    [
                        total[b, pl.ds(k * requests + q, columns, stride=rows), :]
                        for b in range(width // 128)
                    ],
                    axis=1,
                )
                for q in range(requests)
            ],
            axis=0,
        )

    f_copies = []
    for d in (2, 3, 1):
        partial[d] = rows_for(tp_peers[d]).astype(partial.dtype)
        copy = pltpu.make_async_remote_copy(
            src_ref=partial.at[d],
            dst_ref=partial_in.at[d],
            send_sem=f_send.at[d],
            recv_sem=f_recv.at[d],
            device_id=(dp, tp_peers[d]),
            device_id_type=MESH,
        )
        copy.start()
        f_copies.append((d, copy))
    summed = rows_for(tp)
    for d, copy in reversed(f_copies):
        copy.wait_recv()
        summed = summed + partial_in[d].astype(jnp.float32)

    for q in range(requests):
        piece[:, q, :] = summed[q * columns : (q + 1) * columns]
    g_copies = []
    for d in (4, 3, 5, 2, 6, 1, 7):
        to = lax.rem(dp + d, columns)
        copy = pltpu.make_async_remote_copy(
            src_ref=piece.at[to],
            dst_ref=piece_in.at[dp],
            send_sem=g_send.at[d],
            recv_sem=g_recv.at[d],
            device_id=(to, tp),
            device_id_type=MESH,
        )
        copy.start()
        g_copies.append(copy)
    piece_in[dp] = piece[dp]
    for copy in g_copies:
        copy.wait_recv()
    for i in range(columns):
        out_ref[:, i * width : (i + 1) * width] = piece_in[i].astype(out_ref.dtype)

    for _, _, copy in b_copies:
        copy.wait_send()
    for copy in d_copies:
        copy.wait_send()
    for _, copy in f_copies:
        copy.wait_send()
    for copy in g_copies:
        copy.wait_send()


def fused(queries, latent_cache, lengths, value_weight, output_weight):
    requests, all_heads, full_width = queries.shape
    slots = latent_cache.shape[1]
    groups = lax.axis_size("tp")
    columns = lax.axis_size("dp")
    heads, latent_width, value_width = value_weight.shape
    width = output_weight.shape[1]
    rows = groups * requests
    lanes = heads * value_width // 2 // chunk_count
    bf16, f32 = jnp.bfloat16, jnp.float32
    dma = pltpu.SemaphoreType.DMA
    in_hbm = pl.BlockSpec(memory_space=pltpu.HBM)
    return pl.pallas_call(
        kernel,
        out_shape=jax.ShapeDtypeStruct((requests, columns * width), bf16),
        in_specs=[pl.BlockSpec(memory_space=pltpu.SMEM)] + [in_hbm] * 4,
        out_specs=pl.BlockSpec(memory_space=pltpu.VMEM),
        scratch_shapes=[
            pltpu.VMEM((requests, full_width, all_heads), bf16),
            pltpu.VMEM((requests, all_heads, full_width), bf16),
            pltpu.VMEM((requests, full_width, slots), bf16),
            pltpu.VMEM(value_weight.shape, bf16),
            pltpu.VMEM(output_weight.shape, bf16),
            pltpu.VMEM((requests, groups, heads, latent_width), bf16),
            pltpu.VMEM((groups, requests, heads, latent_width), bf16),
            pltpu.VMEM((latent_width // 128, rows * heads, 128), f32),
            pltpu.VMEM((chunk_count, columns, 2 * rows, lanes), bf16),
            pltpu.VMEM((width // 128, columns * rows, 128), f32),
            pltpu.VMEM((groups, requests * columns, width), bf16),
            pltpu.VMEM((groups, requests * columns, width), bf16),
            pltpu.VMEM((columns, requests, width), f32),
            pltpu.VMEM((columns, requests, width), f32),
            dma((2 * requests + 2,)),
            dma((requests, groups)),
            dma((requests, groups)),
            dma((chunk_count, 7)),
            dma((chunk_count, 7)),
            dma((groups,)),
            dma((groups,)),
            dma((columns,)),
            dma((columns,)),
        ],
        compiler_params=pltpu.CompilerParams(
            collective_id=0, has_side_effects=True, vmem_limit_bytes=63 * 1024 * 1024
        ),
        cost_estimate=pl.CostEstimate(
            flops=2 * rows * heads * latent_width * value_width
            + 2 * rows * columns * heads * value_width * width
            + 4 * requests * all_heads * slots * full_width,
            bytes_accessed=2 * (value_weight.size + output_weight.size),
            transcendentals=requests * all_heads * slots,
        ),
    )(
        lengths,
        jnp.swapaxes(queries, 1, 2),
        jnp.swapaxes(latent_cache, 1, 2),
        value_weight,
        output_weight,
    )


def general(queries, latent_cache, lengths, value_weight, output_weight):
    latent_width = value_weight.shape[1]
    scores = (
        jnp.einsum("rhe,rje->rhj", queries, latent_cache, preferred_element_type=jnp.float32)
        * score_scale
    )
    alive_mask = lax.broadcasted_iota(jnp.int32, scores.shape, 2) < lengths[:, None, None]
    scores = jnp.where(alive_mask, scores, -1e30)
    row_max = jnp.max(scores, axis=2, keepdims=True)
    powers = jnp.exp(scores - row_max)
    weights = (powers / jnp.sum(powers, axis=2, keepdims=True)).astype(jnp.bfloat16)
    mixture = jnp.einsum("rhj,rje->rhe", weights, latent_cache, preferred_element_type=jnp.float32)
    latent = mixture[:, :, :latent_width].astype(jnp.bfloat16)
    requests = queries.shape[0]
    groups = lax.axis_size("tp")
    columns = lax.axis_size("dp")
    swapped = lax.all_to_all(latent, "tp", split_axis=1, concat_axis=0, tiled=True)
    values = jnp.einsum("nhd,hde->nhe", swapped, value_weight, preferred_element_type=jnp.float32)
    values = values.astype(jnp.bfloat16).reshape(groups, requests, -1)
    everyone = lax.all_gather(values, "dp", axis=1, tiled=True)
    all_values = everyone.reshape(groups * columns * requests, -1)
    summed = lax.psum_scatter(
        jnp.dot(all_values, output_weight, preferred_element_type=jnp.float32),
        "tp",
        scatter_dimension=0,
        tiled=True,
    )
    rounded = summed.astype(jnp.bfloat16)
    return lax.all_to_all(rounded, "dp", split_axis=0, concat_axis=1, tiled=True)


def solution(mesh):
    fits = mesh.shape["dp"] == 8 and mesh.shape["tp"] == 4
    return jax.shard_map(
        fused if fits else general,
        mesh=mesh,
        in_specs=(
            P(("dp", "tp"), None, None),
            P(("dp", "tp"), None, None),
            P(("dp", "tp")),
            P("tp", None, None),
            P("tp", "dp"),
        ),
        out_specs=P(("dp", "tp"), None),
        check_vma=False,
    )
```

```python
import functools

import jax
import jax.numpy as jnp
from jax import lax
from jax.experimental import pallas as pl
from jax.experimental.pallas import tpu as pltpu
from jax.sharding import PartitionSpec as P

score_scale = 192.0 ** (-0.5)
MESH = pl.DeviceIdType.MESH
chunk_count = 4
part_count = 2


def attend(queries, caches, lengths, latent_width):
    scores, alive = [], []
    for query, cache_t, length in zip(queries, caches, lengths):
        scores.append(jnp.dot(query, cache_t, preferred_element_type=jnp.float32) * score_scale)
        alive.append(lax.broadcasted_iota(jnp.int32, scores[-1].shape, 1) < length)
    scores = jnp.stack([jnp.where(a, s, -1e30) for a, s in zip(alive, scores)])
    powers = jnp.exp(scores - jnp.max(scores, axis=2, keepdims=True))
    weights = (powers / jnp.sum(powers, axis=2, keepdims=True)).astype(jnp.bfloat16)
    return [
        lax.dot_general(
            weights[q],
            cache_t[:latent_width],
            (((1,), (1,)), ((), ())),
            preferred_element_type=jnp.float32,
        ).astype(jnp.bfloat16)
        for q, cache_t in enumerate(caches)
    ]


def kernel(
    lengths_ref,
    query_hbm,
    cache_hbm,
    value_hbm,
    output_hbm,
    out_ref,
    query,
    query_rows,
    cache,
    value_weight,
    output_weight,
    latent_out,
    latent_in,
    latent_wide,
    gathered,
    total,
    partial,
    partial_in,
    piece,
    piece_in,
    load_sem,
    b_send,
    b_recv,
    d_send,
    d_recv,
    f_send,
    f_recv,
    g_send,
    g_recv,
):
    dp = lax.axis_index("dp")
    tp = lax.axis_index("tp")
    requests, groups, parts, _, latent_width = latent_out.shape
    heads = value_weight.shape[0]
    chunks, columns, rows2, lanes = gathered.shape
    value_width = value_weight.shape[2]
    per_chunk = heads // 2 // chunks
    width = output_weight.shape[1]
    rows = groups * requests

    tp_peers = [None, tp + 1 - 2 * lax.rem(tp, 2), lax.rem(tp + 2, 4), 3 - tp]
    across = dp + 1 - 2 * lax.rem(dp, 2)

    loads = []
    for q in range(requests):
        loads.append(pltpu.make_async_copy(cache_hbm.at[q], cache.at[q], load_sem.at[2 * q]))
        loads.append(pltpu.make_async_copy(query_hbm.at[q], query.at[q], load_sem.at[2 * q + 1]))
    load_value = pltpu.make_async_copy(value_hbm, value_weight, load_sem.at[2 * requests])
    load_output = pltpu.make_async_copy(output_hbm, output_weight, load_sem.at[2 * requests + 1])
    for copy in loads:
        copy.start()
    load_value.start()
    load_output.start()

    barrier = pltpu.get_barrier_semaphore()
    for d in (1, 2, 3):
        pl.semaphore_signal(barrier, inc=1, device_id=(dp, tp_peers[d]), device_id_type=MESH)
    for d in range(1, columns):
        pl.semaphore_signal(
            barrier, inc=1, device_id=(lax.rem(dp + d, columns), tp), device_id_type=MESH
        )

    for copy in loads:
        copy.wait()
    for q in range(requests):
        query_rows[q] = query[q].T
    part = heads // parts
    b_copies = {}
    for near in (False, True):
        side = tp // 2 if near else 1 - tp // 2
        first_group = side * (groups // 2)
        first_head = pl.multiple_of(first_group * heads, groups // 2 * heads)
        latents = attend(
            [query_rows[q, pl.ds(first_head, groups // 2 * heads), :] for q in range(requests)],
            [cache[q] for q in range(requests)],
            [lengths_ref[q] for q in range(requests)],
            latent_width,
        )
        for q in range(requests):
            latent_out[q, pl.ds(first_group, groups // 2)] = latents[q].reshape(
                groups // 2, parts, part, latent_width
            )
        if not near:
            pl.semaphore_wait(barrier, groups - 1 + columns - 1)
        for h in range(parts):
            for q in range(requests):
                for d in (1,) if near else (2, 3):
                    copy = pltpu.make_async_remote_copy(
                        src_ref=latent_out.at[q, tp_peers[d], h],
                        dst_ref=latent_in.at[d, q, h],
                        send_sem=b_send.at[h, q, d],
                        recv_sem=b_recv.at[h, q, d],
                        device_id=(dp, tp_peers[d]),
                        device_id_type=MESH,
                    )
                    copy.start()
                    b_copies[h, d, q] = copy

    def widen(block, h, k, q):
        first = pl.multiple_of(((h * groups + k) * requests + q) * part, part)
        for b in range(latent_width // 128):
            latent_wide[b, pl.ds(first, part), :] = block[:, b * 128 : (b + 1) * 128].astype(
                jnp.float32
            )

    def take_part(h):
        for q in range(requests):
            widen(latent_out.at[q, tp, h], h, tp, q)
        for d in (1, 2, 3):
            for q in range(requests):
                b_copies[h, d, q].wait_recv()
                widen(latent_in.at[d, q, h], h, tp_peers[d], q)

    load_value.wait()

    def project(head):
        rows_of = jnp.concatenate(
            [
                latent_wide[b, pl.ds(head // part * rows * part + head % part, rows, stride=part), :]
                for b in range(latent_width // 128)
            ],
            axis=1,
        )
        return jnp.dot(
            rows_of.astype(jnp.bfloat16), value_weight[head], preferred_element_type=jnp.float32
        )

    def value_copy(c, s, slot, device):
        return pltpu.make_async_remote_copy(
            src_ref=gathered.at[c, s],
            dst_ref=gathered.at[c, s],
            send_sem=d_send.at[c, slot],
            recv_sem=d_recv.at[c, slot],
            device_id=(device, tp),
            device_id_type=MESH,
        )

    d_copies = []
    for c in range(chunks):
        if c * parts % chunks == 0:
            take_part(c * parts // chunks)
        for i in range(per_chunk):
            head = 2 * c * per_chunk + i
            pair = jnp.concatenate([project(head), project(head + per_chunk)], axis=0)
            gathered[c, dp, :, i * value_width : (i + 1) * value_width] = pair.astype(jnp.bfloat16)
        for dz in (2, 1, 3):
            copy = value_copy(c, dp, dz, lax.rem(dp + 2 * dz, columns))
            copy.start()
            d_copies.append(copy)
        copy = value_copy(c, dp, 0, across)
        copy.start()
        d_copies.append(copy)

    load_output.wait()

    def hand_on(c):
        for dz in (1, 3, 2):
            source = lax.rem(dp + columns - 2 * dz, columns)
            value_copy(c, source, dz, across).wait_recv()
            copy = value_copy(c, source, 3 + dz, across)
            copy.start()
            d_copies.append(copy)

    hand_on(0)
    for c in range(chunks):
        if c + 1 < chunks:
            hand_on(c + 1)
        for slot in (0, 4, 6, 5):
            value_copy(c, across, slot, across).wait_recv()
        block = gathered[c].reshape(columns * rows2, lanes)
        low = jnp.dot(
            block,
            output_weight[2 * c * lanes : (2 * c + 1) * lanes],
            preferred_element_type=jnp.float32,
        )
        high = jnp.dot(
            block,
            output_weight[(2 * c + 1) * lanes : (2 * c + 2) * lanes],
            preferred_element_type=jnp.float32,
        )
        low = low.reshape(columns, rows2, width)[:, :rows]
        high = high.reshape(columns, rows2, width)[:, rows:]
        term = (low + high).reshape(columns * rows, width)
        for b in range(width // 128):
            if c == 0:
                total[b] = term[:, b * 128 : (b + 1) * 128]
            else:
                total[b] += term[:, b * 128 : (b + 1) * 128]

    def rows_for(k):
        return jnp.concatenate(
            [
                jnp.concatenate(
                    [
                        total[b, pl.ds(k * requests + q, columns, stride=rows), :]
                        for b in range(width // 128)
                    ],
                    axis=1,
                )
                for q in range(requests)
            ],
            axis=0,
        )

    f_copies = []
    for d in (2, 3, 1):
        partial[d] = rows_for(tp_peers[d]).astype(partial.dtype)
        copy = pltpu.make_async_remote_copy(
            src_ref=partial.at[d],
            dst_ref=partial_in.at[d],
            send_sem=f_send.at[d],
            recv_sem=f_recv.at[d],
            device_id=(dp, tp_peers[d]),
            device_id_type=MESH,
        )
        copy.start()
        f_copies.append((d, copy))
    summed = rows_for(tp)
    for d, copy in reversed(f_copies):
        copy.wait_recv()
        summed = summed + partial_in[d].astype(jnp.float32)

    for q in range(requests):
        piece[:, q, :] = summed[q * columns : (q + 1) * columns]
    g_copies = []
    for d in (4, 3, 5, 2, 6, 1, 7):
        to = lax.rem(dp + d, columns)
        copy = pltpu.make_async_remote_copy(
            src_ref=piece.at[to],
            dst_ref=piece_in.at[dp],
            send_sem=g_send.at[d],
            recv_sem=g_recv.at[d],
            device_id=(to, tp),
            device_id_type=MESH,
        )
        copy.start()
        g_copies.append(copy)
    piece_in[dp] = piece[dp]
    for copy in g_copies:
        copy.wait_recv()
    for i in range(columns):
        out_ref[:, i * width : (i + 1) * width] = piece_in[i].astype(out_ref.dtype)

    for copy in b_copies.values():
        copy.wait_send()
    for copy in d_copies:
        copy.wait_send()
    for _, copy in f_copies:
        copy.wait_send()
    for copy in g_copies:
        copy.wait_send()


def fused(queries, latent_cache, lengths, value_weight, output_weight):
    requests, all_heads, full_width = queries.shape
    slots = latent_cache.shape[1]
    groups = lax.axis_size("tp")
    columns = lax.axis_size("dp")
    heads, latent_width, value_width = value_weight.shape
    width = output_weight.shape[1]
    rows = groups * requests
    lanes = heads * value_width // 2 // chunk_count
    bf16, f32 = jnp.bfloat16, jnp.float32
    dma = pltpu.SemaphoreType.DMA
    in_hbm = pl.BlockSpec(memory_space=pltpu.HBM)
    return pl.pallas_call(
        kernel,
        out_shape=jax.ShapeDtypeStruct((requests, columns * width), bf16),
        in_specs=[pl.BlockSpec(memory_space=pltpu.SMEM)] + [in_hbm] * 4,
        out_specs=pl.BlockSpec(memory_space=pltpu.VMEM),
        scratch_shapes=[
            pltpu.VMEM((requests, full_width, all_heads), bf16),
            pltpu.VMEM((requests, all_heads, full_width), bf16),
            pltpu.VMEM((requests, full_width, slots), bf16),
            pltpu.VMEM(value_weight.shape, bf16),
            pltpu.VMEM(output_weight.shape, bf16),
            pltpu.VMEM((requests, groups, part_count, heads // part_count, latent_width), bf16),
            pltpu.VMEM((groups, requests, part_count, heads // part_count, latent_width), bf16),
            pltpu.VMEM((latent_width // 128, rows * heads, 128), f32),
            pltpu.VMEM((chunk_count, columns, 2 * rows, lanes), bf16),
            pltpu.VMEM((width // 128, columns * rows, 128), f32),
            pltpu.VMEM((groups, requests * columns, width), bf16),
            pltpu.VMEM((groups, requests * columns, width), bf16),
            pltpu.VMEM((columns, requests, width), f32),
            pltpu.VMEM((columns, requests, width), f32),
            dma((2 * requests + 2,)),
            dma((part_count, requests, groups)),
            dma((part_count, requests, groups)),
            dma((chunk_count, 7)),
            dma((chunk_count, 7)),
            dma((groups,)),
            dma((groups,)),
            dma((columns,)),
            dma((columns,)),
        ],
        compiler_params=pltpu.CompilerParams(
            collective_id=0, has_side_effects=True, vmem_limit_bytes=63 * 1024 * 1024
        ),
        cost_estimate=pl.CostEstimate(
            flops=2 * rows * heads * latent_width * value_width
            + 2 * rows * columns * heads * value_width * width
            + 4 * requests * all_heads * slots * full_width,
            bytes_accessed=2 * (value_weight.size + output_weight.size),
            transcendentals=requests * all_heads * slots,
        ),
    )(
        lengths,
        jnp.swapaxes(queries, 1, 2),
        jnp.swapaxes(latent_cache, 1, 2),
        value_weight,
        output_weight,
    )


def general(queries, latent_cache, lengths, value_weight, output_weight):
    latent_width = value_weight.shape[1]
    scores = (
        jnp.einsum("rhe,rje->rhj", queries, latent_cache, preferred_element_type=jnp.float32)
        * score_scale
    )
    alive_mask = lax.broadcasted_iota(jnp.int32, scores.shape, 2) < lengths[:, None, None]
    scores = jnp.where(alive_mask, scores, -1e30)
    row_max = jnp.max(scores, axis=2, keepdims=True)
    powers = jnp.exp(scores - row_max)
    weights = (powers / jnp.sum(powers, axis=2, keepdims=True)).astype(jnp.bfloat16)
    mixture = jnp.einsum("rhj,rje->rhe", weights, latent_cache, preferred_element_type=jnp.float32)
    latent = mixture[:, :, :latent_width].astype(jnp.bfloat16)
    requests = queries.shape[0]
    groups = lax.axis_size("tp")
    columns = lax.axis_size("dp")
    swapped = lax.all_to_all(latent, "tp", split_axis=1, concat_axis=0, tiled=True)
    values = jnp.einsum("nhd,hde->nhe", swapped, value_weight, preferred_element_type=jnp.float32)
    values = values.astype(jnp.bfloat16).reshape(groups, requests, -1)
    everyone = lax.all_gather(values, "dp", axis=1, tiled=True)
    all_values = everyone.reshape(groups * columns * requests, -1)
    summed = lax.psum_scatter(
        jnp.dot(all_values, output_weight, preferred_element_type=jnp.float32),
        "tp",
        scatter_dimension=0,
        tiled=True,
    )
    rounded = summed.astype(jnp.bfloat16)
    return lax.all_to_all(rounded, "dp", split_axis=0, concat_axis=1, tiled=True)


def solution(mesh):
    fits = mesh.shape["dp"] == 8 and mesh.shape["tp"] == 4
    return jax.shard_map(
        fused if fits else general,
        mesh=mesh,
        in_specs=(
            P(("dp", "tp"), None, None),
            P(("dp", "tp"), None, None),
            P(("dp", "tp")),
            P("tp", None, None),
            P("tp", "dp"),
        ),
        out_specs=P(("dp", "tp"), None),
        check_vma=False,
    )
```

```python
import functools

import jax
import jax.numpy as jnp
from jax import lax
from jax.experimental import pallas as pl
from jax.experimental.pallas import tpu as pltpu
from jax.sharding import PartitionSpec as P

score_scale = 192.0 ** (-0.5)
MESH = pl.DeviceIdType.MESH
chunk_count = 4
part_count = 2


def attend(queries, caches, lengths, latent_width):
    scores, alive = [], []
    for query, cache_t, length in zip(queries, caches, lengths):
        scores.append(jnp.dot(query, cache_t, preferred_element_type=jnp.float32) * score_scale)
        alive.append(lax.broadcasted_iota(jnp.int32, scores[-1].shape, 1) < length)
    scores = jnp.stack([jnp.where(a, s, -1e30) for a, s in zip(alive, scores)])
    powers = jnp.exp(scores - jnp.max(scores, axis=2, keepdims=True))
    weights = (powers / jnp.sum(powers, axis=2, keepdims=True)).astype(jnp.bfloat16)
    return [
        lax.dot_general(
            weights[q],
            cache_t[:latent_width],
            (((1,), (1,)), ((), ())),
            preferred_element_type=jnp.float32,
        ).astype(jnp.bfloat16)
        for q, cache_t in enumerate(caches)
    ]


def kernel(
    lengths_ref,
    query_hbm,
    cache_hbm,
    value_hbm,
    output_hbm,
    out_ref,
    query,
    query_rows,
    cache,
    value_weight,
    output_weight,
    latent_out,
    latent_in,
    latent_wide,
    gathered,
    total,
    partial,
    partial_in,
    piece,
    load_sem,
    b_send,
    b_recv,
    d_send,
    d_recv,
    f_send,
    f_recv,
):
    dp = lax.axis_index("dp")
    tp = lax.axis_index("tp")
    requests, groups, parts, _, latent_width = latent_out.shape
    heads = value_weight.shape[0]
    chunks, columns, rows2, lanes = gathered.shape
    value_width = value_weight.shape[2]
    per_chunk = heads // 2 // chunks
    width = output_weight.shape[1]
    rows = groups * requests

    tp_peers = [None, tp + 1 - 2 * lax.rem(tp, 2), lax.rem(tp + 2, 4), 3 - tp]
    across = dp + 1 - 2 * lax.rem(dp, 2)

    loads = []
    for q in range(requests):
        loads.append(pltpu.make_async_copy(cache_hbm.at[q], cache.at[q], load_sem.at[2 * q]))
        loads.append(pltpu.make_async_copy(query_hbm.at[q], query.at[q], load_sem.at[2 * q + 1]))
    load_value = pltpu.make_async_copy(value_hbm, value_weight, load_sem.at[2 * requests])
    load_output = pltpu.make_async_copy(output_hbm, output_weight, load_sem.at[2 * requests + 1])
    for copy in loads:
        copy.start()
    load_value.start()
    load_output.start()

    barrier = pltpu.get_barrier_semaphore()
    for dj in range(columns):
        for dk in range(groups):
            if dj or dk:
                pl.semaphore_signal(
                    barrier,
                    inc=1,
                    device_id=(lax.rem(dp + dj, columns), tp_peers[dk] if dk else tp),
                    device_id_type=MESH,
                )
    total[width // 128 * columns * rows :] = jnp.zeros(
        ((8 - width // 128) * columns * rows, 128), jnp.float32
    )

    for copy in loads:
        copy.wait()
    for q in range(requests):
        query_rows[q] = query[q].T
    part = heads // parts
    b_copies = {}
    for near in (False, True):
        side = tp // 2 if near else 1 - tp // 2
        first_group = side * (groups // 2)
        first_head = pl.multiple_of(first_group * heads, groups // 2 * heads)
        latents = attend(
            [query_rows[q, pl.ds(first_head, groups // 2 * heads), :] for q in range(requests)],
            [cache[q] for q in range(requests)],
            [lengths_ref[q] for q in range(requests)],
            latent_width,
        )
        for q in range(requests):
            latent_out[q, pl.ds(first_group, groups // 2)] = latents[q].reshape(
                groups // 2, parts, part, latent_width
            )
        if not near:
            pl.semaphore_wait(barrier, groups * columns - 1)
        for h in range(parts):
            for q in range(requests):
                for d in (1,) if near else (2, 3):
                    copy = pltpu.make_async_remote_copy(
                        src_ref=latent_out.at[q, tp_peers[d], h],
                        dst_ref=latent_in.at[d, q, h],
                        send_sem=b_send.at[h, q, d],
                        recv_sem=b_recv.at[h, q, d],
                        device_id=(dp, tp_peers[d]),
                        device_id_type=MESH,
                    )
                    copy.start()
                    b_copies[h, d, q] = copy

    def widen(block, h, k, q):
        first = pl.multiple_of(((h * groups + k) * requests + q) * part, part)
        for b in range(latent_width // 128):
            latent_wide[b, pl.ds(first, part), :] = block[:, b * 128 : (b + 1) * 128].astype(
                jnp.float32
            )

    def take_part(h):
        for q in range(requests):
            widen(latent_out.at[q, tp, h], h, tp, q)
        for d in (1, 2, 3):
            for q in range(requests):
                b_copies[h, d, q].wait_recv()
                widen(latent_in.at[d, q, h], h, tp_peers[d], q)

    load_value.wait()

    def project(head):
        rows_of = jnp.concatenate(
            [
                latent_wide[b, pl.ds(head // part * rows * part + head % part, rows, stride=part), :]
                for b in range(latent_width // 128)
            ],
            axis=1,
        )
        return jnp.dot(
            rows_of.astype(jnp.bfloat16), value_weight[head], preferred_element_type=jnp.float32
        )

    def value_copy(c, s, slot, device):
        return pltpu.make_async_remote_copy(
            src_ref=gathered.at[c, s],
            dst_ref=gathered.at[c, s],
            send_sem=d_send.at[c, slot],
            recv_sem=d_recv.at[c, slot],
            device_id=(device, tp),
            device_id_type=MESH,
        )

    d_copies = []
    for c in range(chunks):
        if c * parts % chunks == 0:
            take_part(c * parts // chunks)
        for i in range(per_chunk):
            head = 2 * c * per_chunk + i
            pair = jnp.concatenate([project(head), project(head + per_chunk)], axis=0)
            gathered[c, dp, :, i * value_width : (i + 1) * value_width] = pair.astype(jnp.bfloat16)
        for dz in (2, 1, 3):
            copy = value_copy(c, dp, dz, lax.rem(dp + 2 * dz, columns))
            copy.start()
            d_copies.append(copy)
        copy = value_copy(c, dp, 0, across)
        copy.start()
        d_copies.append(copy)

    load_output.wait()

    def hand_on(c):
        for dz in (1, 3, 2):
            source = lax.rem(dp + columns - 2 * dz, columns)
            value_copy(c, source, dz, across).wait_recv()
            copy = value_copy(c, source, 3 + dz, across)
            copy.start()
            d_copies.append(copy)

    hand_on(0)
    for c in range(chunks):
        if c + 1 < chunks:
            hand_on(c + 1)
        for slot in (0, 4, 6, 5):
            value_copy(c, across, slot, across).wait_recv()
        block = gathered[c].reshape(columns * rows2, lanes)
        low = jnp.dot(
            block,
            output_weight[2 * c * lanes : (2 * c + 1) * lanes],
            preferred_element_type=jnp.float32,
        )
        high = jnp.dot(
            block,
            output_weight[(2 * c + 1) * lanes : (2 * c + 2) * lanes],
            preferred_element_type=jnp.float32,
        )
        low = low.reshape(columns, rows2, width)[:, :rows]
        high = high.reshape(columns, rows2, width)[:, rows:]
        term = (low + high).reshape(columns * rows, width)
        for b in range(width // 128):
            at = slice(b * columns * rows, (b + 1) * columns * rows)
            if c == 0:
                total[at] = term[:, b * 128 : (b + 1) * 128]
            else:
                total[at] += term[:, b * 128 : (b + 1) * 128]

    for to in range(columns * groups):
        partial[to] = jnp.concatenate(
            [
                total[pl.ds(to * requests + q, 8, stride=columns * rows), :]
                for q in range(requests)
            ],
            axis=0,
        ).astype(partial.dtype)
    me = dp * groups + tp
    f_copies = []
    for dj in (4, 3, 5, 2, 6, 1, 7, 0):
        for dk in (2, 3, 1, 0):
            if dj == 0 and dk == 0:
                continue
            to_dp = lax.rem(dp + dj, columns)
            to_tp = tp_peers[dk] if dk else tp
            copy = pltpu.make_async_remote_copy(
                src_ref=partial.at[to_dp * groups + to_tp],
                dst_ref=partial_in.at[me],
                send_sem=f_send.at[dj * groups + dk],
                recv_sem=f_recv.at[dj * groups + dk],
                device_id=(to_dp, to_tp),
                device_id_type=MESH,
            )
            copy.start()
            f_copies.append(copy)
    partial_in[me] = partial[me]
    for copy in f_copies:
        copy.wait_recv()
    for i in range(columns):
        summed = partial_in[i * groups].astype(jnp.float32)
        for g in range(1, groups):
            summed = summed + partial_in[i * groups + g].astype(jnp.float32)
        piece[i * 16 : (i + 1) * 16] = summed
    for i in range(columns):
        for b in range(width // 128):
            first = i * width + b * 128
            out_ref[:, first : first + 128] = piece[pl.ds(i * 16 + b, requests, stride=8), :].astype(
                out_ref.dtype
            )

    for copy in b_copies.values():
        copy.wait_send()
    for copy in d_copies:
        copy.wait_send()
    for copy in f_copies:
        copy.wait_send()


def fused(queries, latent_cache, lengths, value_weight, output_weight):
    requests, all_heads, full_width = queries.shape
    slots = latent_cache.shape[1]
    groups = lax.axis_size("tp")
    columns = lax.axis_size("dp")
    heads, latent_width, value_width = value_weight.shape
    width = output_weight.shape[1]
    rows = groups * requests
    lanes = heads * value_width // 2 // chunk_count
    bf16, f32 = jnp.bfloat16, jnp.float32
    dma = pltpu.SemaphoreType.DMA
    in_hbm = pl.BlockSpec(memory_space=pltpu.HBM)
    return pl.pallas_call(
        kernel,
        out_shape=jax.ShapeDtypeStruct((requests, columns * width), bf16),
        in_specs=[pl.BlockSpec(memory_space=pltpu.SMEM)] + [in_hbm] * 4,
        out_specs=pl.BlockSpec(memory_space=pltpu.VMEM),
        scratch_shapes=[
            pltpu.VMEM((requests, full_width, all_heads), bf16),
            pltpu.VMEM((requests, all_heads, full_width), bf16),
            pltpu.VMEM((requests, full_width, slots), bf16),
            pltpu.VMEM(value_weight.shape, bf16),
            pltpu.VMEM(output_weight.shape, bf16),
            pltpu.VMEM((requests, groups, part_count, heads // part_count, latent_width), bf16),
            pltpu.VMEM((groups, requests, part_count, heads // part_count, latent_width), bf16),
            pltpu.VMEM((latent_width // 128, rows * heads, 128), f32),
            pltpu.VMEM((chunk_count, columns, 2 * rows, lanes), bf16),
            pltpu.VMEM((8 * columns * rows, 128), f32),
            pltpu.VMEM((columns * groups, 16, 128), bf16),
            pltpu.VMEM((columns * groups, 16, 128), bf16),
            pltpu.VMEM((columns * 16, 128), f32),
            dma((2 * requests + 2,)),
            dma((part_count, requests, groups)),
            dma((part_count, requests, groups)),
            dma((chunk_count, 7)),
            dma((chunk_count, 7)),
            dma((columns * groups,)),
            dma((columns * groups,)),
        ],
        compiler_params=pltpu.CompilerParams(
            collective_id=0, has_side_effects=True, vmem_limit_bytes=63 * 1024 * 1024
        ),
        cost_estimate=pl.CostEstimate(
            flops=2 * rows * heads * latent_width * value_width
            + 2 * rows * columns * heads * value_width * width
            + 4 * requests * all_heads * slots * full_width,
            bytes_accessed=2 * (value_weight.size + output_weight.size),
            transcendentals=requests * all_heads * slots,
        ),
    )(
        lengths,
        jnp.swapaxes(queries, 1, 2),
        jnp.swapaxes(latent_cache, 1, 2),
        value_weight,
        output_weight,
    )


def general(queries, latent_cache, lengths, value_weight, output_weight):
    latent_width = value_weight.shape[1]
    scores = (
        jnp.einsum("rhe,rje->rhj", queries, latent_cache, preferred_element_type=jnp.float32)
        * score_scale
    )
    alive_mask = lax.broadcasted_iota(jnp.int32, scores.shape, 2) < lengths[:, None, None]
    scores = jnp.where(alive_mask, scores, -1e30)
    row_max = jnp.max(scores, axis=2, keepdims=True)
    powers = jnp.exp(scores - row_max)
    weights = (powers / jnp.sum(powers, axis=2, keepdims=True)).astype(jnp.bfloat16)
    mixture = jnp.einsum("rhj,rje->rhe", weights, latent_cache, preferred_element_type=jnp.float32)
    latent = mixture[:, :, :latent_width].astype(jnp.bfloat16)
    requests = queries.shape[0]
    groups = lax.axis_size("tp")
    columns = lax.axis_size("dp")
    swapped = lax.all_to_all(latent, "tp", split_axis=1, concat_axis=0, tiled=True)
    values = jnp.einsum("nhd,hde->nhe", swapped, value_weight, preferred_element_type=jnp.float32)
    values = values.astype(jnp.bfloat16).reshape(groups, requests, -1)
    everyone = lax.all_gather(values, "dp", axis=1, tiled=True)
    all_values = everyone.reshape(groups * columns * requests, -1)
    summed = lax.psum_scatter(
        jnp.dot(all_values, output_weight, preferred_element_type=jnp.float32),
        "tp",
        scatter_dimension=0,
        tiled=True,
    )
    rounded = summed.astype(jnp.bfloat16)
    return lax.all_to_all(rounded, "dp", split_axis=0, concat_axis=1, tiled=True)


def solution(mesh):
    fits = mesh.shape["dp"] == 8 and mesh.shape["tp"] == 4
    return jax.shard_map(
        fused if fits else general,
        mesh=mesh,
        in_specs=(
            P(("dp", "tp"), None, None),
            P(("dp", "tp"), None, None),
            P(("dp", "tp")),
            P("tp", None, None),
            P("tp", "dp"),
        ),
        out_specs=P(("dp", "tp"), None),
        check_vma=False,
    )
```

```python
import functools

import jax
import jax.numpy as jnp
from jax import lax
from jax.experimental import pallas as pl
from jax.experimental.pallas import tpu as pltpu
from jax.sharding import PartitionSpec as P

score_scale = 192.0 ** (-0.5)
MESH = pl.DeviceIdType.MESH
chunk_count = 4
part_count = 2


def attend(queries, caches, lengths, latent_width):
    scores, alive = [], []
    for query, cache_t, length in zip(queries, caches, lengths):
        scores.append(jnp.dot(query, cache_t, preferred_element_type=jnp.float32) * score_scale)
        alive.append(lax.broadcasted_iota(jnp.int32, scores[-1].shape, 1) < length)
    scores = jnp.stack([jnp.where(a, s, -1e30) for a, s in zip(alive, scores)])
    powers = jnp.exp(scores - jnp.max(scores, axis=2, keepdims=True))
    weights = (powers / jnp.sum(powers, axis=2, keepdims=True)).astype(jnp.bfloat16)
    return [
        lax.dot_general(
            weights[q],
            cache_t[:latent_width],
            (((1,), (1,)), ((), ())),
            preferred_element_type=jnp.float32,
        ).astype(jnp.bfloat16)
        for q, cache_t in enumerate(caches)
    ]


def kernel(
    lengths_ref,
    query_hbm,
    cache_hbm,
    value_hbm,
    output_hbm,
    out_ref,
    query,
    query_rows,
    cache,
    value_weight,
    output_weight,
    latent_out,
    latent_in,
    latent_wide,
    gathered,
    total,
    partial,
    partial_in,
    piece,
    load_sem,
    b_send,
    b_recv,
    d_send,
    d_recv,
    f_send,
    f_recv,
):
    dp = lax.axis_index("dp")
    tp = lax.axis_index("tp")
    requests, groups, parts, _, latent_width = latent_out.shape
    heads = value_weight.shape[0]
    chunks, columns, rows2, lanes = gathered.shape
    value_width = value_weight.shape[2]
    per_chunk = heads // 2 // chunks
    width = output_weight.shape[1]
    rows = groups * requests

    tp_peers = [None, tp + 1 - 2 * lax.rem(tp, 2), lax.rem(tp + 2, 4), 3 - tp]
    across = dp + 1 - 2 * lax.rem(dp, 2)

    loads = []
    for q in range(requests):
        loads.append(pltpu.make_async_copy(cache_hbm.at[q], cache.at[q], load_sem.at[2 * q]))
        loads.append(pltpu.make_async_copy(query_hbm.at[q], query.at[q], load_sem.at[2 * q + 1]))
    load_value = pltpu.make_async_copy(value_hbm, value_weight, load_sem.at[2 * requests])
    load_output = pltpu.make_async_copy(output_hbm, output_weight, load_sem.at[2 * requests + 1])
    for copy in loads:
        copy.start()
    load_value.start()
    load_output.start()

    barrier = pltpu.get_barrier_semaphore()
    for dj in range(columns):
        for dk in range(groups):
            if dj or dk:
                pl.semaphore_signal(
                    barrier,
                    inc=1,
                    device_id=(lax.rem(dp + dj, columns), tp_peers[dk] if dk else tp),
                    device_id_type=MESH,
                )
    total[width // 128 * columns * rows :] = jnp.zeros(
        ((8 - width // 128) * columns * rows, 128), jnp.float32
    )

    for copy in loads:
        copy.wait()
    for q in range(requests):
        query_rows[q] = query[q].T
    part = heads // parts
    b_copies = {}
    for near in (False, True):
        side = tp // 2 if near else 1 - tp // 2
        first_group = side * (groups // 2)
        first_head = pl.multiple_of(first_group * heads, groups // 2 * heads)
        latents = attend(
            [query_rows[q, pl.ds(first_head, groups // 2 * heads), :] for q in range(requests)],
            [cache[q] for q in range(requests)],
            [lengths_ref[q] for q in range(requests)],
            latent_width,
        )
        for q in range(requests):
            latent_out[q, pl.ds(first_group, groups // 2)] = latents[q].reshape(
                groups // 2, parts, part, latent_width
            )
        if not near:
            pl.semaphore_wait(barrier, groups * columns - 1)
        for h in range(parts):
            for q in range(requests):
                for d in (1,) if near else (2, 3):
                    copy = pltpu.make_async_remote_copy(
                        src_ref=latent_out.at[q, tp_peers[d], h],
                        dst_ref=latent_in.at[d, q, h],
                        send_sem=b_send.at[h, q, d],
                        recv_sem=b_recv.at[h, q, d],
                        device_id=(dp, tp_peers[d]),
                        device_id_type=MESH,
                    )
                    copy.start()
                    b_copies[h, d, q] = copy

    def widen(block, h, k, q):
        first = pl.multiple_of(((h * groups + k) * requests + q) * part, part)
        for b in range(latent_width // 128):
            latent_wide[b, pl.ds(first, part), :] = block[:, b * 128 : (b + 1) * 128].astype(
                jnp.float32
            )

    def take_part(h):
        for q in range(requests):
            widen(latent_out.at[q, tp, h], h, tp, q)
        for d in (1, 2, 3):
            for q in range(requests):
                b_copies[h, d, q].wait_recv()
                widen(latent_in.at[d, q, h], h, tp_peers[d], q)

    load_value.wait()

    def project(head):
        rows_of = jnp.concatenate(
            [
                latent_wide[b, pl.ds(head // part * rows * part + head % part, rows, stride=part), :]
                for b in range(latent_width // 128)
            ],
            axis=1,
        )
        return jnp.dot(
            rows_of.astype(jnp.bfloat16), value_weight[head], preferred_element_type=jnp.float32
        )

    z, z_size = dp // 2, columns // 2
    d_copies = []

    def value_copy(c, s, way):
        device = (across, dp + 2, dp - 2)[way]
        return pltpu.make_async_remote_copy(
            src_ref=gathered.at[c, s],
            dst_ref=gathered.at[c, s],
            send_sem=d_send.at[c, s, way],
            recv_sem=d_recv.at[c, s],
            device_id=(device, tp),
            device_id_type=MESH,
        )

    def send(c, s, way, condition):
        copy = value_copy(c, s, way)
        d_copies.append((condition, copy))
        pl.when(condition)(copy.start)

    def sibling(s):
        return s + 1 - 2 * lax.rem(dp, 2)

    def x_first(c):
        return c % 2 == 1

    def wave(w):
        for c in range(max(0, w - z_size + 1), min(chunks, w)):
            if w - c == 1 and x_first(c):
                value_copy(c, across, 0).wait_recv()
                send(c, across, 1, z < z_size - 1)
                send(c, across, 2, z > 0)
            d = w - c
            for way in (1, 2):
                near = dp - 2 * d if way == 1 else dp + 2 * d
                present = z >= d if way == 1 else z + d < z_size
                further = present & (z < z_size - 1) if way == 1 else present & (z > 0)
                for s in (near, sibling(near)) if x_first(c) else (near,):
                    pl.when(present)(value_copy(c, s, 0).wait_recv)
                    send(c, s, way, further)
                    if not x_first(c):
                        send(c, s, 0, present)

    def rest(c):
        if not x_first(c):
            for d in range(z_size):
                value_copy(c, lax.rem(across + 2 * d, columns), 0).wait_recv()

    for c in range(chunks):
        if c * parts % chunks == 0:
            take_part(c * parts // chunks)
        for i in range(per_chunk):
            head = 2 * c * per_chunk + i
            pair = jnp.concatenate([project(head), project(head + per_chunk)], axis=0)
            gathered[c, dp, :, i * value_width : (i + 1) * value_width] = pair.astype(jnp.bfloat16)
        send(c, dp, 0, z >= 0)
        send(c, dp, 1, z < z_size - 1)
        send(c, dp, 2, z > 0)
        if c >= 2:
            wave(c - 1)

    load_output.wait()

    for w in range(chunks - 1, z_size):
        wave(w)
    for c in range(chunks):
        if c < chunks - 1:
            wave(c + z_size)
        rest(c)
        block = gathered[c].reshape(columns * rows2, lanes)
        low = jnp.dot(
            block,
            output_weight[2 * c * lanes : (2 * c + 1) * lanes],
            preferred_element_type=jnp.float32,
        )
        high = jnp.dot(
            block,
            output_weight[(2 * c + 1) * lanes : (2 * c + 2) * lanes],
            preferred_element_type=jnp.float32,
        )
        low = low.reshape(columns, rows2, width)[:, :rows]
        high = high.reshape(columns, rows2, width)[:, rows:]
        term = (low + high).reshape(columns * rows, width)
        for b in range(width // 128):
            at = slice(b * columns * rows, (b + 1) * columns * rows)
            if c == 0:
                total[at] = term[:, b * 128 : (b + 1) * 128]
            else:
                total[at] += term[:, b * 128 : (b + 1) * 128]

    for to in range(columns * groups):
        partial[to] = jnp.concatenate(
            [
                total[pl.ds(to * requests + q, 8, stride=columns * rows), :]
                for q in range(requests)
            ],
            axis=0,
        ).astype(partial.dtype)
    me = dp * groups + tp
    f_copies = []
    for dj in (4, 3, 5, 2, 6, 1, 7, 0):
        for dk in (2, 3, 1, 0):
            if dj == 0 and dk == 0:
                continue
            to_dp = lax.rem(dp + dj, columns)
            to_tp = tp_peers[dk] if dk else tp
            copy = pltpu.make_async_remote_copy(
                src_ref=partial.at[to_dp * groups + to_tp],
                dst_ref=partial_in.at[me],
                send_sem=f_send.at[dj * groups + dk],
                recv_sem=f_recv.at[dj * groups + dk],
                device_id=(to_dp, to_tp),
                device_id_type=MESH,
            )
            copy.start()
            f_copies.append(copy)
    partial_in[me] = partial[me]
    for copy in f_copies:
        copy.wait_recv()
    for i in range(columns):
        summed = partial_in[i * groups].astype(jnp.float32)
        for g in range(1, groups):
            summed = summed + partial_in[i * groups + g].astype(jnp.float32)
        piece[i * 16 : (i + 1) * 16] = summed
    for i in range(columns):
        for b in range(width // 128):
            first = i * width + b * 128
            out_ref[:, first : first + 128] = piece[pl.ds(i * 16 + b, requests, stride=8), :].astype(
                out_ref.dtype
            )

    for copy in b_copies.values():
        copy.wait_send()
    for condition, copy in d_copies:
        pl.when(condition)(copy.wait_send)
    for copy in f_copies:
        copy.wait_send()


def fused(queries, latent_cache, lengths, value_weight, output_weight):
    requests, all_heads, full_width = queries.shape
    slots = latent_cache.shape[1]
    groups = lax.axis_size("tp")
    columns = lax.axis_size("dp")
    heads, latent_width, value_width = value_weight.shape
    width = output_weight.shape[1]
    rows = groups * requests
    lanes = heads * value_width // 2 // chunk_count
    bf16, f32 = jnp.bfloat16, jnp.float32
    dma = pltpu.SemaphoreType.DMA
    in_hbm = pl.BlockSpec(memory_space=pltpu.HBM)
    return pl.pallas_call(
        kernel,
        out_shape=jax.ShapeDtypeStruct((requests, columns * width), bf16),
        in_specs=[pl.BlockSpec(memory_space=pltpu.SMEM)] + [in_hbm] * 4,
        out_specs=pl.BlockSpec(memory_space=pltpu.VMEM),
        scratch_shapes=[
            pltpu.VMEM((requests, full_width, all_heads), bf16),
            pltpu.VMEM((requests, all_heads, full_width), bf16),
            pltpu.VMEM((requests, full_width, slots), bf16),
            pltpu.VMEM(value_weight.shape, bf16),
            pltpu.VMEM(output_weight.shape, bf16),
            pltpu.VMEM((requests, groups, part_count, heads // part_count, latent_width), bf16),
            pltpu.VMEM((groups, requests, part_count, heads // part_count, latent_width), bf16),
            pltpu.VMEM((latent_width // 128, rows * heads, 128), f32),
            pltpu.VMEM((chunk_count, columns, 2 * rows, lanes), bf16),
            pltpu.VMEM((8 * columns * rows, 128), f32),
            pltpu.VMEM((columns * groups, 16, 128), bf16),
            pltpu.VMEM((columns * groups, 16, 128), bf16),
            pltpu.VMEM((columns * 16, 128), f32),
            dma((2 * requests + 2,)),
            dma((part_count, requests, groups)),
            dma((part_count, requests, groups)),
            dma((chunk_count, columns, 3)),
            dma((chunk_count, columns)),
            dma((columns * groups,)),
            dma((columns * groups,)),
        ],
        compiler_params=pltpu.CompilerParams(
            collective_id=0, has_side_effects=True, vmem_limit_bytes=63 * 1024 * 1024
        ),
        cost_estimate=pl.CostEstimate(
            flops=2 * rows * heads * latent_width * value_width
            + 2 * rows * columns * heads * value_width * width
            + 4 * requests * all_heads * slots * full_width,
            bytes_accessed=2 * (value_weight.size + output_weight.size),
            transcendentals=requests * all_heads * slots,
        ),
    )(
        lengths,
        jnp.swapaxes(queries, 1, 2),
        jnp.swapaxes(latent_cache, 1, 2),
        value_weight,
        output_weight,
    )


def general(queries, latent_cache, lengths, value_weight, output_weight):
    latent_width = value_weight.shape[1]
    scores = (
        jnp.einsum("rhe,rje->rhj", queries, latent_cache, preferred_element_type=jnp.float32)
        * score_scale
    )
    alive_mask = lax.broadcasted_iota(jnp.int32, scores.shape, 2) < lengths[:, None, None]
    scores = jnp.where(alive_mask, scores, -1e30)
    row_max = jnp.max(scores, axis=2, keepdims=True)
    powers = jnp.exp(scores - row_max)
    weights = (powers / jnp.sum(powers, axis=2, keepdims=True)).astype(jnp.bfloat16)
    mixture = jnp.einsum("rhj,rje->rhe", weights, latent_cache, preferred_element_type=jnp.float32)
    latent = mixture[:, :, :latent_width].astype(jnp.bfloat16)
    requests = queries.shape[0]
    groups = lax.axis_size("tp")
    columns = lax.axis_size("dp")
    swapped = lax.all_to_all(latent, "tp", split_axis=1, concat_axis=0, tiled=True)
    values = jnp.einsum("nhd,hde->nhe", swapped, value_weight, preferred_element_type=jnp.float32)
    values = values.astype(jnp.bfloat16).reshape(groups, requests, -1)
    everyone = lax.all_gather(values, "dp", axis=1, tiled=True)
    all_values = everyone.reshape(groups * columns * requests, -1)
    summed = lax.psum_scatter(
        jnp.dot(all_values, output_weight, preferred_element_type=jnp.float32),
        "tp",
        scatter_dimension=0,
        tiled=True,
    )
    rounded = summed.astype(jnp.bfloat16)
    return lax.all_to_all(rounded, "dp", split_axis=0, concat_axis=1, tiled=True)


def solution(mesh):
    fits = mesh.shape["dp"] == 8 and mesh.shape["tp"] == 4
    return jax.shard_map(
        fused if fits else general,
        mesh=mesh,
        in_specs=(
            P(("dp", "tp"), None, None),
            P(("dp", "tp"), None, None),
            P(("dp", "tp")),
            P("tp", None, None),
            P("tp", "dp"),
        ),
        out_specs=P(("dp", "tp"), None),
        check_vma=False,
    )
```

```python
import functools

import jax
import jax.numpy as jnp
from jax import lax
from jax.experimental import pallas as pl
from jax.experimental.pallas import tpu as pltpu
from jax.sharding import PartitionSpec as P

score_scale = 192.0 ** (-0.5)
MESH = pl.DeviceIdType.MESH
chunk_count = 4
part_count = 2


def attend(queries, caches, lengths, latent_width):
    scores, alive = [], []
    for query, cache_t, length in zip(queries, caches, lengths):
        scores.append(jnp.dot(query, cache_t, preferred_element_type=jnp.float32) * score_scale)
        alive.append(lax.broadcasted_iota(jnp.int32, scores[-1].shape, 1) < length)
    scores = jnp.stack([jnp.where(a, s, -1e30) for a, s in zip(alive, scores)])
    powers = jnp.exp(scores - jnp.max(scores, axis=2, keepdims=True))
    weights = (powers / jnp.sum(powers, axis=2, keepdims=True)).astype(jnp.bfloat16)
    return [
        lax.dot_general(
            weights[q],
            cache_t[:latent_width],
            (((1,), (1,)), ((), ())),
            preferred_element_type=jnp.float32,
        ).astype(jnp.bfloat16)
        for q, cache_t in enumerate(caches)
    ]


def kernel(
    lengths_ref,
    query_hbm,
    cache_hbm,
    value_hbm,
    output_hbm,
    out_ref,
    query,
    query_rows,
    cache,
    value_weight,
    output_weight,
    latent_out,
    latent_in,
    latent_wide,
    gathered,
    total,
    partial,
    partial_in,
    piece,
    load_sem,
    b_send,
    b_recv,
    d_send,
    d_recv,
    f_send,
    f_recv,
):
    dp = lax.axis_index("dp")
    tp = lax.axis_index("tp")
    requests, groups, parts, _, latent_width = latent_out.shape
    heads = value_weight.shape[0]
    chunks, columns, rows2, lanes = gathered.shape
    value_width = value_weight.shape[2]
    per_chunk = heads // 2 // chunks
    width = output_weight.shape[1]
    rows = groups * requests

    tp_peers = [None, tp + 1 - 2 * lax.rem(tp, 2), lax.rem(tp + 2, 4), 3 - tp]

    loads = []
    for q in range(requests):
        loads.append(pltpu.make_async_copy(cache_hbm.at[q], cache.at[q], load_sem.at[2 * q]))
        loads.append(pltpu.make_async_copy(query_hbm.at[q], query.at[q], load_sem.at[2 * q + 1]))
    load_value = pltpu.make_async_copy(value_hbm, value_weight, load_sem.at[2 * requests])
    load_output = pltpu.make_async_copy(output_hbm, output_weight, load_sem.at[2 * requests + 1])
    for copy in loads:
        copy.start()
    load_value.start()
    load_output.start()

    barrier = pltpu.get_barrier_semaphore()
    for dj in range(columns):
        for dk in range(groups):
            if dj or dk:
                pl.semaphore_signal(
                    barrier,
                    inc=1,
                    device_id=(lax.rem(dp + dj, columns), tp_peers[dk] if dk else tp),
                    device_id_type=MESH,
                )
    total[width // 128 * columns * rows :] = jnp.zeros(
        ((8 - width // 128) * columns * rows, 128), jnp.float32
    )

    for copy in loads:
        copy.wait()
    for q in range(requests):
        query_rows[q] = query[q].T
    part = heads // parts
    b_copies = {}
    for near in (False, True):
        side = tp // 2 if near else 1 - tp // 2
        first_group = side * (groups // 2)
        first_head = pl.multiple_of(first_group * heads, groups // 2 * heads)
        latents = attend(
            [query_rows[q, pl.ds(first_head, groups // 2 * heads), :] for q in range(requests)],
            [cache[q] for q in range(requests)],
            [lengths_ref[q] for q in range(requests)],
            latent_width,
        )
        for q in range(requests):
            latent_out[q, pl.ds(first_group, groups // 2)] = latents[q].reshape(
                groups // 2, parts, part, latent_width
            )
        if not near:
            pl.semaphore_wait(barrier, groups * columns - 1)
        for h in range(parts):
            for q in range(requests):
                for d in (1,) if near else (2, 3):
                    copy = pltpu.make_async_remote_copy(
                        src_ref=latent_out.at[q, tp_peers[d], h],
                        dst_ref=latent_in.at[d, q, h],
                        send_sem=b_send.at[h, q, d],
                        recv_sem=b_recv.at[h, q, d],
                        device_id=(dp, tp_peers[d]),
                        device_id_type=MESH,
                    )
                    copy.start()
                    b_copies[h, d, q] = copy

    def widen(block, h, k, q):
        first = pl.multiple_of(((h * groups + k) * requests + q) * part, part)
        for b in range(latent_width // 128):
            latent_wide[b, pl.ds(first, part), :] = block[:, b * 128 : (b + 1) * 128].astype(
                jnp.float32
            )

    def take_part(h):
        for q in range(requests):
            widen(latent_out.at[q, tp, h], h, tp, q)
        for d in (1, 2, 3):
            for q in range(requests):
                b_copies[h, d, q].wait_recv()
                widen(latent_in.at[d, q, h], h, tp_peers[d], q)

    load_value.wait()

    def project(head):
        rows_of = jnp.concatenate(
            [
                latent_wide[b, pl.ds(head // part * rows * part + head % part, rows, stride=part), :]
                for b in range(latent_width // 128)
            ],
            axis=1,
        )
        return jnp.dot(
            rows_of.astype(jnp.bfloat16), value_weight[head], preferred_element_type=jnp.float32
        )

    def value_copy(c, s, slot, device):
        return pltpu.make_async_remote_copy(
            src_ref=gathered.at[c, s],
            dst_ref=gathered.at[c, s],
            send_sem=d_send.at[c, slot],
            recv_sem=d_recv.at[c, slot],
            device_id=(device, tp),
            device_id_type=MESH,
        )

    d_copies = []
    for c in range(chunks):
        if c * parts % chunks == 0:
            take_part(c * parts // chunks)
        for i in range(per_chunk):
            head = 2 * c * per_chunk + i
            pair = jnp.concatenate([project(head), project(head + per_chunk)], axis=0)
            gathered[c, dp, :, i * value_width : (i + 1) * value_width] = pair.astype(jnp.bfloat16)
        for d in (4, 3, 5, 2, 6, 1, 7):
            copy = value_copy(c, dp, d - 1, lax.rem(dp + d, columns))
            copy.start()
            d_copies.append(copy)

    load_output.wait()

    for c in range(chunks):
        for d in range(1, columns):
            source = lax.rem(dp + columns - d, columns)
            value_copy(c, source, d - 1, source).wait_recv()
        block = gathered[c].reshape(columns * rows2, lanes)
        low = jnp.dot(
            block,
            output_weight[2 * c * lanes : (2 * c + 1) * lanes],
            preferred_element_type=jnp.float32,
        )
        high = jnp.dot(
            block,
            output_weight[(2 * c + 1) * lanes : (2 * c + 2) * lanes],
            preferred_element_type=jnp.float32,
        )
        low = low.reshape(columns, rows2, width)[:, :rows]
        high = high.reshape(columns, rows2, width)[:, rows:]
        term = (low + high).reshape(columns * rows, width)
        for b in range(width // 128):
            at = slice(b * columns * rows, (b + 1) * columns * rows)
            if c == 0:
                total[at] = term[:, b * 128 : (b + 1) * 128]
            else:
                total[at] += term[:, b * 128 : (b + 1) * 128]

    for to in range(columns * groups):
        partial[to] = jnp.concatenate(
            [
                total[pl.ds(to * requests + q, 8, stride=columns * rows), :]
                for q in range(requests)
            ],
            axis=0,
        ).astype(partial.dtype)
    me = dp * groups + tp
    f_copies = []
    for dj in (4, 3, 5, 2, 6, 1, 7, 0):
        for dk in (2, 3, 1, 0):
            if dj == 0 and dk == 0:
                continue
            to_dp = lax.rem(dp + dj, columns)
            to_tp = tp_peers[dk] if dk else tp
            copy = pltpu.make_async_remote_copy(
                src_ref=partial.at[to_dp * groups + to_tp],
                dst_ref=partial_in.at[me],
                send_sem=f_send.at[dj * groups + dk],
                recv_sem=f_recv.at[dj * groups + dk],
                device_id=(to_dp, to_tp),
                device_id_type=MESH,
            )
            copy.start()
            f_copies.append(copy)
    partial_in[me] = partial[me]
    for copy in f_copies:
        copy.wait_recv()
    for i in range(columns):
        summed = partial_in[i * groups].astype(jnp.float32)
        for g in range(1, groups):
            summed = summed + partial_in[i * groups + g].astype(jnp.float32)
        piece[i * 16 : (i + 1) * 16] = summed
    for i in range(columns):
        for b in range(width // 128):
            first = i * width + b * 128
            out_ref[:, first : first + 128] = piece[pl.ds(i * 16 + b, requests, stride=8), :].astype(
                out_ref.dtype
            )

    for copy in b_copies.values():
        copy.wait_send()
    for copy in d_copies:
        copy.wait_send()
    for copy in f_copies:
        copy.wait_send()


def fused(queries, latent_cache, lengths, value_weight, output_weight):
    requests, all_heads, full_width = queries.shape
    slots = latent_cache.shape[1]
    groups = lax.axis_size("tp")
    columns = lax.axis_size("dp")
    heads, latent_width, value_width = value_weight.shape
    width = output_weight.shape[1]
    rows = groups * requests
    lanes = heads * value_width // 2 // chunk_count
    bf16, f32 = jnp.bfloat16, jnp.float32
    dma = pltpu.SemaphoreType.DMA
    in_hbm = pl.BlockSpec(memory_space=pltpu.HBM)
    return pl.pallas_call(
        kernel,
        out_shape=jax.ShapeDtypeStruct((requests, columns * width), bf16),
        in_specs=[pl.BlockSpec(memory_space=pltpu.SMEM)] + [in_hbm] * 4,
        out_specs=pl.BlockSpec(memory_space=pltpu.VMEM),
        scratch_shapes=[
            pltpu.VMEM((requests, full_width, all_heads), bf16),
            pltpu.VMEM((requests, all_heads, full_width), bf16),
            pltpu.VMEM((requests, full_width, slots), bf16),
            pltpu.VMEM(value_weight.shape, bf16),
            pltpu.VMEM(output_weight.shape, bf16),
            pltpu.VMEM((requests, groups, part_count, heads // part_count, latent_width), bf16),
            pltpu.VMEM((groups, requests, part_count, heads // part_count, latent_width), bf16),
            pltpu.VMEM((latent_width // 128, rows * heads, 128), f32),
            pltpu.VMEM((chunk_count, columns, 2 * rows, lanes), bf16),
            pltpu.VMEM((8 * columns * rows, 128), f32),
            pltpu.VMEM((columns * groups, 16, 128), bf16),
            pltpu.VMEM((columns * groups, 16, 128), bf16),
            pltpu.VMEM((columns * 16, 128), f32),
            dma((2 * requests + 2,)),
            dma((part_count, requests, groups)),
            dma((part_count, requests, groups)),
            dma((chunk_count, 7)),
            dma((chunk_count, 7)),
            dma((columns * groups,)),
            dma((columns * groups,)),
        ],
        compiler_params=pltpu.CompilerParams(
            collective_id=0, has_side_effects=True, vmem_limit_bytes=63 * 1024 * 1024
        ),
        cost_estimate=pl.CostEstimate(
            flops=2 * rows * heads * latent_width * value_width
            + 2 * rows * columns * heads * value_width * width
            + 4 * requests * all_heads * slots * full_width,
            bytes_accessed=2 * (value_weight.size + output_weight.size),
            transcendentals=requests * all_heads * slots,
        ),
    )(
        lengths,
        jnp.swapaxes(queries, 1, 2),
        jnp.swapaxes(latent_cache, 1, 2),
        value_weight,
        output_weight,
    )


def general(queries, latent_cache, lengths, value_weight, output_weight):
    latent_width = value_weight.shape[1]
    scores = (
        jnp.einsum("rhe,rje->rhj", queries, latent_cache, preferred_element_type=jnp.float32)
        * score_scale
    )
    alive_mask = lax.broadcasted_iota(jnp.int32, scores.shape, 2) < lengths[:, None, None]
    scores = jnp.where(alive_mask, scores, -1e30)
    row_max = jnp.max(scores, axis=2, keepdims=True)
    powers = jnp.exp(scores - row_max)
    weights = (powers / jnp.sum(powers, axis=2, keepdims=True)).astype(jnp.bfloat16)
    mixture = jnp.einsum("rhj,rje->rhe", weights, latent_cache, preferred_element_type=jnp.float32)
    latent = mixture[:, :, :latent_width].astype(jnp.bfloat16)
    requests = queries.shape[0]
    groups = lax.axis_size("tp")
    columns = lax.axis_size("dp")
    swapped = lax.all_to_all(latent, "tp", split_axis=1, concat_axis=0, tiled=True)
    values = jnp.einsum("nhd,hde->nhe", swapped, value_weight, preferred_element_type=jnp.float32)
    values = values.astype(jnp.bfloat16).reshape(groups, requests, -1)
    everyone = lax.all_gather(values, "dp", axis=1, tiled=True)
    all_values = everyone.reshape(groups * columns * requests, -1)
    summed = lax.psum_scatter(
        jnp.dot(all_values, output_weight, preferred_element_type=jnp.float32),
        "tp",
        scatter_dimension=0,
        tiled=True,
    )
    rounded = summed.astype(jnp.bfloat16)
    return lax.all_to_all(rounded, "dp", split_axis=0, concat_axis=1, tiled=True)


def solution(mesh):
    fits = mesh.shape["dp"] == 8 and mesh.shape["tp"] == 4
    return jax.shard_map(
        fused if fits else general,
        mesh=mesh,
        in_specs=(
            P(("dp", "tp"), None, None),
            P(("dp", "tp"), None, None),
            P(("dp", "tp")),
            P("tp", None, None),
            P("tp", "dp"),
        ),
        out_specs=P(("dp", "tp"), None),
        check_vma=False,
    )
```
